256 devices in a mesh: tile: 32 (over z, y), lev: 8 (over x, core).
Axes of the slice: x: 4, y: 4, z: 8, core: 2. Of those that a mesh axis runs over, the one named last changes fastest.
Arguments:
- members: bfloat16 [32, 65536, 128], P('lev', 'tile'), may hold values from -4 to 4
- obs_operator: bfloat16 [8, 2048, 4, 128, 128], P('lev', 'tile'), as said below
- col_level: int32 [8, 2048, 4], P('lev', 'tile'), may hold values from 0 to 3
- col_block: int32 [8, 2048, 4], P('lev', 'tile'), may hold values from 0 to 19, as said below
- obs_count: int32 [2048], P(('tile', 'lev')), may hold values from 1 to 128, as said below
- obs_values: float32 [2048, 128], P(('tile', 'lev')), may hold values from -60 to 60
- obs_weight: float32 [2048, 128], P(('tile', 'lev')), may hold values from 0.01 to 0.18
Outputs:
- analysed: bfloat16 [32, 65536, 128], P('lev', 'tile')
- transform: float32 [128, 128], replicated
The draws below stay inside these ranges and needn't reach their ends.
Inputs may be any that keep to these rules, and one draw needn't show every extreme that they name: `col_block`: for the observation block in position i of its tile (i < 64), every column block lies within 2 of i * 16 // 64 + 2, and never names a block outside the grid. `obs_count`: the first block of every tile uses all 128 rows. `obs_operator`: entries lie within 4 / sqrt(8192) of zero.
All inputs are finite; a program needn't handle non-finite values.
Results may differ from the reference program's by a relative error of at most 0.0076.
Values may be sent and summed in bfloat16 or wider, within the bound.
No kernel may reach another device: no remote copies, remote signals or barrier semaphores. Data moves between devices by JAX's collectives and lax.ppermute only.
A program may use at most 128 MiB of HBM per device.

```python
import math
import jax
import jax.numpy as jnp
from jax import lax

MEMBERS = 128
BLK = 128
NNZ = 4
HALO = 2
LEV_DEV = 4
HC_DEV = 2048
OB_TILE = 64
HB_DEV = 16
WIN_BLK = 20
GROUPS = 8
LEVELS = 32
HCELLS = 65536
OBLK = 2048


def draw_members(key, part):
    key = jax.random.fold_in(key, 3)
    common_key, own_key = jax.random.split(key)
    common = jax.random.truncated_normal(common_key, -4.0, 4.0, (HCELLS, MEMBERS), jnp.float32)

    def level_draw(level):
        own = jax.random.truncated_normal(jax.random.fold_in(own_key, level), -4.0, 4.0, (HCELLS, MEMBERS), jnp.float32)
        return jnp.clip(0.70710678 * (common + own), -4.0, 4.0).astype(jnp.bfloat16)
    return lax.map(level_draw, jnp.arange(LEVELS, dtype=jnp.int32))


def draw_obs_operator(key, part):
    key = jax.random.fold_in(key, 13)
    common_key, own_key = jax.random.split(key)
    scale = (2.0 * GROUPS * NNZ * BLK) ** (-0.5)
    common = jax.random.truncated_normal(common_key, -4.0, 4.0, (OBLK, NNZ, BLK, BLK), jnp.float32)

    def group_draw(group):
        own = jax.random.truncated_normal(jax.random.fold_in(own_key, group), -4.0, 4.0, (OBLK, NNZ, BLK, BLK), jnp.float32)
        return (scale * jnp.clip(0.70710678 * (common + own), -4.0, 4.0)).astype(jnp.bfloat16)
    return lax.map(group_draw, jnp.arange(GROUPS, dtype=jnp.int32))


def draw_col_block(key, part):
    key = jax.random.fold_in(key, 5)
    own_key, shared_key, pick_key = jax.random.split(key, 3)
    own_offsets = jax.random.randint(own_key, (GROUPS, OBLK, NNZ), -HALO, HALO + 1, dtype=jnp.int32)
    shared_offsets = jax.random.randint(shared_key, (1, OBLK, NNZ), -HALO, HALO + 1, dtype=jnp.int32)
    own_pick = jax.random.randint(pick_key, (GROUPS, OBLK, NNZ), 0, 4, dtype=jnp.int32) == 0
    offsets = jnp.where(own_pick, own_offsets, shared_offsets)
    blocks = jnp.arange(OBLK, dtype=jnp.int32)
    tile_of = blocks // OB_TILE
    position = blocks % OB_TILE
    center = position * HB_DEV // OB_TILE + HALO
    lowest = jnp.where(tile_of == 0, HALO, 0)
    highest = jnp.where(tile_of == OBLK // OB_TILE - 1, HB_DEV + HALO - 1, HB_DEV + 2 * HALO - 1)
    picked = center[None, :, None] + offsets
    picked = jnp.minimum(jnp.maximum(picked, lowest[None, :, None]), highest[None, :, None])
    return picked.astype(jnp.int32)


def draw_obs_count(key, part):
    key = jax.random.fold_in(key, 7)
    counts = jax.random.randint(key, (OBLK,), 1, BLK + 1, dtype=jnp.int32)
    return counts.at[::OB_TILE].set(BLK).astype(jnp.int32)


def draw_obs_weight(key, part):
    key = jax.random.fold_in(key, 11)
    unit = jax.random.uniform(key, (OBLK, BLK), jnp.float32)
    base = jnp.exp(jnp.log(0.01) + unit * jnp.log(10.0))
    ramp = jnp.sqrt(1.0 + 2.0 * jnp.arange(OBLK, dtype=jnp.float32) / OBLK)
    return (base * ramp[:, None]).astype(jnp.float32)


def place_ends(result, key, least, largest):
    shape = result.shape
    index_at = [jax.random.randint(jax.random.fold_in(key, axis), (), 0, shape[axis]) for axis in range(len(shape))]
    result = result.at[tuple(index_at)].set(least)
    longest = shape.index(max(shape))
    index_at[longest] = (index_at[longest] + 1) % shape[longest]
    return result.at[tuple(index_at)].set(largest)


def block_scale(key, extent, cuts, low, top_value):
    def one(axis_at, parts):
        heights = jax.random.uniform(jax.random.fold_in(jax.random.fold_in(key, 6), axis_at), (parts,), jnp.float32, low / len(cuts), top_value / len(cuts))
        return jnp.repeat(jnp.exp(heights), extent[axis_at] // parts).reshape((-1,) + (1,) * (len(extent) - axis_at - 1))

    gain = one(*cuts[0])
    for cut in cuts[1:]:
        gain = gain * one(*cut)
    return gain


def gaussian(stream_key, extent, width, bound, cuts=(), kind=jnp.bfloat16):
    entries = jax.random.normal(stream_key, extent, jnp.float32) * width
    if len(cuts) > 0:
        entries = block_scale(stream_key, extent, cuts, -0.22, 0.18) * entries
    return jnp.clip(entries, min=-bound, max=bound).astype(kind)


def setup_inputs(seed: int = 0) -> dict:
    key_list = jax.random.split(jax.random.key(seed), 8)
    return {
        "members": draw_members(jax.random.fold_in(key_list[7], 71), 0),
        "obs_operator": draw_obs_operator(jax.random.fold_in(key_list[7], 71), 0),
        "col_level": place_ends(jax.random.randint(key_list[2], (GROUPS, OBLK, NNZ), 0, LEV_DEV), jax.random.fold_in(key_list[2], 1), 0, LEV_DEV - 1).astype(jnp.int32),
        "col_block": draw_col_block(jax.random.fold_in(key_list[7], 71), 0),
        "obs_count": draw_obs_count(jax.random.fold_in(key_list[7], 71), 0),
        "obs_values": gaussian(key_list[5], (OBLK, BLK), 10.0, 60.0, ((0, 256),), jnp.float32),
        "obs_weight": draw_obs_weight(jax.random.fold_in(key_list[7], 71), 0),
    }


def observe_tile(tile_id, padded, obs_operator, col_level, col_block):
    window = lax.dynamic_slice_in_dim(padded, tile_id * HC_DEV, HC_DEV + 2 * HALO * BLK, 1)
    window = window.reshape(LEVELS, WIN_BLK, BLK, MEMBERS).reshape(LEVELS * WIN_BLK, BLK, MEMBERS)
    op_blocks = lax.dynamic_slice_in_dim(obs_operator, tile_id * OB_TILE, OB_TILE, 1)
    level_pick = lax.dynamic_slice_in_dim(col_level, tile_id * OB_TILE, OB_TILE, 1)
    block_pick = lax.dynamic_slice_in_dim(col_block, tile_id * OB_TILE, OB_TILE, 1)
    group_base = (jnp.arange(GROUPS, dtype=jnp.int32) * LEV_DEV)[:, None, None]
    flat_index = ((group_base + level_pick) * WIN_BLK + block_pick).astype(jnp.int32)
    chosen = window[flat_index]
    return jnp.einsum('gokij,gokjm->oim', op_blocks.astype(jnp.float32), chosen.astype(jnp.float32), precision=lax.Precision.HIGHEST)

def reference(members, obs_operator, col_level, col_block, obs_count, obs_values, obs_weight):
    highest = lax.Precision.HIGHEST
    padded = jnp.pad(members, ((0, 0), (HALO * BLK, HALO * BLK), (0, 0)))
    tile_count = OBLK // OB_TILE
    observed = lax.map(lambda tile_id: observe_tile(tile_id, padded, obs_operator, col_level, col_block), jnp.arange(tile_count, dtype=jnp.int32))
    observed = observed.reshape(OBLK, BLK, MEMBERS)
    live_rows = (jnp.arange(BLK, dtype=jnp.int32)[None, :] < obs_count[:, None]).astype(jnp.float32)
    weight = obs_weight * live_rows
    mean_obs = lax.optimization_barrier(jnp.sum(observed, axis=2)) / MEMBERS
    row_scale = weight / math.sqrt(MEMBERS - 1)
    spread = ((observed - mean_obs[:, :, None]) * row_scale[:, :, None]).reshape(-1, MEMBERS)
    innovation = ((obs_values - mean_obs) * weight).reshape(-1)
    gram = jnp.dot(spread.T.astype(jnp.float32), spread.astype(jnp.float32), precision=highest, preferred_element_type=jnp.float32)
    pull = jnp.dot(innovation.astype(jnp.float32), spread.astype(jnp.float32), precision=highest, preferred_element_type=jnp.float32)
    identity = jnp.eye(MEMBERS, dtype=jnp.float32)
    lower = jnp.linalg.cholesky(identity + gram)
    inverse = lax.linalg.triangular_solve(lower, identity, left_side=True, lower=True)
    shift_weights = jnp.dot(inverse.T, jnp.dot(inverse, pull, precision=highest), precision=highest)
    transform = shift_weights[:, None] / math.sqrt(MEMBERS - 1) + inverse.T
    transform_bf = transform.astype(jnp.bfloat16)

    def update(level_members):
        row_mean = lax.optimization_barrier(jnp.sum(level_members.astype(jnp.float32), axis=1)) / MEMBERS
        anomalies = (level_members.astype(jnp.float32) - row_mean[:, None]).astype(jnp.bfloat16)
        moved = jnp.dot(anomalies.astype(jnp.float32), transform_bf.astype(jnp.float32), preferred_element_type=jnp.float32)
        return (row_mean[:, None] + moved).astype(jnp.bfloat16)
    analysed = lax.map(update, members)
    return (analysed, transform)
```

```python
import functools
import math

import jax
import jax.numpy as jnp
from jax import lax
from jax.experimental import pallas as pl
from jax.experimental.pallas import tpu as pltpu
from jax.sharding import PartitionSpec as P

BLK = 128
HALO = 2
RIM = HALO * BLK
NNZ = 4
LEVS = 4
CELLS = 2048
OWN = 8
DATA = OWN * BLK
TAIL = 32
ROWS = DATA + TAIL
NEAR = 4 * BLK
EDGE = NEAR + RIM
BF, F32 = jnp.bfloat16, jnp.float32
HIGHEST = lax.Precision.HIGHEST
VMEM = pltpu.VMEM
SMEM = pltpu.SMEM
HBM = pltpu.HBM


def other_core(value):
    return lax.ppermute(value, "lev", [(i, i ^ 1) for i in range(8)])


def x_shift(value, step):
    return lax.ppermute(value, "lev", [(i, (i + 2 * step) % 8) for i in range(8)])


def place(z, y, x, core):
    return (z * 4 + y) * 8 + x * 2 + core


PLANES = [[place(z, y, x, c) for y in range(4) for x in range(4)] for z in range(8) for c in range(2)]
LINES = [[place(z, y, x, c) for z in range(8)] for y in range(4) for x in range(4) for c in range(2)]


def group_sum(value, groups):
    copies = jnp.broadcast_to(value[None], (len(groups[0]),) + value.shape)
    came = lax.all_to_all(copies, ("tile", "lev"), 0, 0, axis_index_groups=groups)
    return jnp.sum(came, axis=0)


def split_means(mean):
    high = mean.astype(BF).astype(F32)
    rest = mean - high
    mid = rest.astype(BF).astype(F32)
    low = rest - mid
    return jnp.concatenate([high, mid, low, jnp.zeros_like(low)], axis=0).astype(BF)


def join_means(tail):
    parts = tail.astype(F32)
    return (parts[0:8] + parts[8:16]) + parts[16:24]


def observe_owner(owner, at_ref, op_ref, window_ref, length, base, out_ref):
    lane = lax.broadcasted_iota(jnp.int32, (BLK, BLK), 1)
    means = jnp.zeros((BLK, BLK), F32)

    def product(j):
        o = owner * OWN + j
        rows = []
        for k in range(NNZ):
            at = (at_ref[0, k, o] // 32) * length + (at_ref[0, k, o] % 32 - base) * BLK
            rows.append(window_ref[pl.ds(pl.multiple_of(at, BLK), BLK), :])
        return jnp.dot(
            jnp.concatenate([op_ref[0, j, k] for k in range(NNZ)], axis=1),
            jnp.concatenate(rows, axis=0),
            preferred_element_type=F32,
        )

    ahead = 1
    parts = [product(j) for j in range(ahead)]
    for j in range(OWN):
        if j + ahead < OWN:
            parts.append(product(j + ahead))
        part = parts[j]
        mean = jnp.sum(part, axis=1, keepdims=True) * (1.0 / BLK)
        out_ref[j * BLK : (j + 1) * BLK, :] = (part - mean).astype(BF)
        means = jnp.where(lane == j, mean, means)
    out_ref[DATA:ROWS, :] = split_means(jnp.transpose(means)[0:OWN])


CHUNKS_IN = 3


def inner_kernel(
    core_ref, at_ref, op_hbm, members_hbm,
    send_ref, keep_ref, edge_ref, rim_ref, held, members_ref, sem, edge_sem, rim_sem, members_sem,
):
    core = core_ref[0]

    def blocks(owner):
        return op_hbm.at[:, pl.ds(owner * OWN, OWN)]

    def owner_of(n):
        parity = 1 - core if n < CHUNKS_IN else core
        return 2 * (n % CHUNKS_IN) + 2 - parity

    loads = [pltpu.make_async_copy(members_hbm, members_ref, members_sem)]
    loads[0].start(priority=1)
    for n in range(2 * CHUNKS_IN):
        loads.append(pltpu.make_async_copy(blocks(owner_of(n)), held.at[n], sem.at[n]))
        loads[-1].start(priority=n % 2)
    edges = [pltpu.make_async_copy(blocks(7 * n), edge_ref.at[n], edge_sem.at[n]) for n in range(2)]
    for n in range(2):
        for v in range(LEVS):
            cells = members_hbm.at[pl.ds(v * CELLS + n * (CELLS - NEAR), NEAR)]
            edges.append(pltpu.make_async_copy(cells, rim_ref.at[n, v], rim_sem.at[n, v]))
    for n, copy in enumerate(edges):
        copy.start(priority=n % 2)
    loads[0].wait()
    for n in range(2 * CHUNKS_IN):
        loads[n + 1].wait()
        out = send_ref if n < CHUNKS_IN else keep_ref
        observe_owner(
            owner_of(n), at_ref, held.at[n], members_ref, CELLS, HALO, out.at[n % CHUNKS_IN]
        )
    for copy in edges:
        copy.wait()


def inner_blocks(core, places, operator, members):
    out = jax.ShapeDtypeStruct((CHUNKS_IN, ROWS, BLK), BF)
    return pl.pallas_call(
        inner_kernel,
        in_specs=[pl.BlockSpec(memory_space=SMEM)] * 2 + [pl.BlockSpec(memory_space=HBM)] * 2,
        out_specs=[pl.BlockSpec(memory_space=VMEM)] * 4,
        out_shape=[
            out,
            out,
            jax.ShapeDtypeStruct((2, 1, OWN, NNZ, BLK, BLK), BF),
            jax.ShapeDtypeStruct((2, LEVS, NEAR, BLK), BF),
        ],
        scratch_shapes=[
            pltpu.VMEM((2 * CHUNKS_IN, 1, OWN, NNZ, BLK, BLK), BF),
            pltpu.VMEM((LEVS * CELLS, BLK), BF),
            pltpu.SemaphoreType.DMA((2 * CHUNKS_IN,)),
            pltpu.SemaphoreType.DMA((2,)),
            pltpu.SemaphoreType.DMA((2, LEVS)),
            pltpu.SemaphoreType.DMA,
        ],
        compiler_params=pltpu.CompilerParams(vmem_limit_bytes=46 * 2**20),
        cost_estimate=pl.CostEstimate(flops=1_000_000, bytes_accessed=2**16, transcendentals=0),
        name="observe_inner",
    )(core, places, operator, members)


def outer_kernel(
    core_ref, at_ref, edge_ref, rim_ref, before_ref, after_ref, send_ref, keep_ref, low, high
):
    for v in range(LEVS):
        low[v * EDGE : v * EDGE + RIM, :] = before_ref[v]
        low[v * EDGE + RIM : (v + 1) * EDGE, :] = rim_ref[0, v]
        high[v * EDGE : (v + 1) * EDGE - RIM, :] = rim_ref[1, v]
        high[(v + 1) * EDGE - RIM : (v + 1) * EDGE, :] = after_ref[v]

    def run(low_out, high_out):
        observe_owner(0, at_ref, edge_ref.at[0], low, EDGE, 0, low_out)
        observe_owner(7, at_ref, edge_ref.at[1], high, EDGE, 14, high_out)

    @pl.when(core_ref[0] == 0)
    def _():
        run(keep_ref, send_ref)

    @pl.when(core_ref[0] == 1)
    def _():
        run(send_ref, keep_ref)


def outer_blocks(core, places, edge, rim, before, after):
    out = jax.ShapeDtypeStruct((ROWS, BLK), BF)
    return pl.pallas_call(
        outer_kernel,
        in_specs=[pl.BlockSpec(memory_space=SMEM)] * 2 + [pl.BlockSpec(memory_space=VMEM)] * 4,
        out_specs=[pl.BlockSpec(memory_space=VMEM)] * 2,
        out_shape=[out, out],
        scratch_shapes=[pltpu.VMEM((LEVS * EDGE, BLK), BF)] * 2,
        compiler_params=pltpu.CompilerParams(vmem_limit_bytes=32 * 2**20),
        cost_estimate=pl.CostEstimate(flops=270_000_000, bytes_accessed=4 * 2**20, transcendentals=0),
        name="observe_outer",
    )(core, places, edge, rim, before, after)


def pair_kernel(core_ref, x_ref, came_ref, keep_ref, came_edge, keep_edge, *outs):
    core = core_ref[0]

    def add(a_ref, b_ref, out_ref):
        out_ref[0:DATA, :] = (a_ref[0:DATA, :].astype(F32) + b_ref[0:DATA, :].astype(F32)).astype(BF)
        out_ref[DATA:ROWS, :] = split_means(join_means(a_ref[DATA:ROWS, :]) + join_means(b_ref[DATA:ROWS, :]))

    for step in range(4):
        x = lax.rem(x_ref[0] + step, 4)

        @pl.when(x == 3 * core)
        def _():
            add(came_edge, keep_edge, outs[step])

        @pl.when(x != 3 * core)
        def _():
            at = jnp.clip(x - 1 + core, 0, CHUNKS_IN - 1)
            add(came_ref.at[at], keep_ref.at[at], outs[step])


def pair_sum(core, x, came, keep, came_edge, keep_edge):
    out = jax.ShapeDtypeStruct((ROWS, BLK), BF)
    return pl.pallas_call(
        pair_kernel,
        in_specs=[pl.BlockSpec(memory_space=SMEM)] * 2 + [pl.BlockSpec(memory_space=VMEM)] * 4,
        out_specs=[pl.BlockSpec(memory_space=VMEM)] * 4,
        out_shape=[out] * 4,
        compiler_params=pltpu.CompilerParams(vmem_limit_bytes=32 * 2**20),
        name="pair_sum",
    )(core, x, came, keep, came_edge, keep_edge)


HALF = BLK // 2


def pack(gram, pull):
    row = lax.broadcasted_iota(jnp.int32, (HALF, BLK), 0)
    lane = lax.broadcasted_iota(jnp.int32, (HALF, BLK), 1)
    upper, lower = gram[0:HALF], gram[HALF:BLK]
    mixed = jnp.where(lane <= row, upper, pltpu.roll(lower, HALF, 1))
    diagonal = jnp.sum(jnp.where(lane == row + HALF, lower, 0.0), axis=0, keepdims=True)
    quarter = HALF // 2
    left = lax.broadcasted_iota(jnp.int32, (quarter, BLK), 1) < HALF
    first = lax.broadcasted_iota(jnp.int32, (8, BLK), 0) == 0

    def fold(square, extra):
        body = jnp.where(left, square[0:quarter], pltpu.roll(square[quarter:HALF], HALF, 1))
        return jnp.concatenate([body, jnp.where(first, extra, 0.0)], axis=0)

    return fold(lower, pull), fold(mixed, diagonal)


def unpack(zero, one):
    row = lax.broadcasted_iota(jnp.int32, (HALF, BLK), 0)
    lane = lax.broadcasted_iota(jnp.int32, (HALF, BLK), 1)
    quarter = HALF // 2
    pull = zero[quarter : quarter + 1]
    diagonal = one[quarter : quarter + 1]

    def unfold(body):
        return jnp.concatenate([body, pltpu.roll(body, HALF, 1)], axis=0)

    corner = unfold(zero[0:quarter])
    mixed = unfold(one[0:quarter])
    above = jnp.where((lane > row) & (lane < HALF), mixed, 0.0)
    top = jnp.where(lane <= row, mixed, 0.0)
    bottom = jnp.where(lane < HALF, corner, 0.0)
    strict = jnp.concatenate(
        [jnp.where(lane < row, mixed, 0.0), bottom + pltpu.roll(above, HALF, 1)], axis=0
    )
    middle = jnp.where(lane == row + HALF, diagonal, 0.0)
    full = jnp.concatenate([top, bottom + middle + pltpu.roll(above, HALF, 1)], axis=0)
    return full + jnp.transpose(strict), pull


def gram_kernel(
    core_ref, count_ref, a_ref, b_ref, c_ref, d_ref, values_ref, weight_ref, send_ref, keep_ref
):
    parts = (a_ref, b_ref, c_ref, d_ref)
    mean = sum(join_means(ref[DATA:ROWS, :]) for ref in parts)
    row = lax.broadcasted_iota(jnp.int32, (OWN, BLK), 0)
    lane = lax.broadcasted_iota(jnp.int32, (OWN, BLK), 1)
    count = jnp.zeros((OWN, BLK), jnp.int32)
    for j in range(OWN):
        count = jnp.where(row == j, count_ref[j], count)
    weight = jnp.where(lane < count, weight_ref[...], 0.0)
    innovation = (values_ref[...] - mean) * weight
    scale = weight * (1.0 / math.sqrt(BLK - 1))
    columns = jnp.transpose(
        jnp.concatenate([scale, innovation, jnp.zeros((BLK - 2 * OWN, BLK), F32)], axis=0)
    )
    gram = jnp.zeros((BLK, BLK), F32)
    pull = jnp.zeros((1, BLK), F32)
    for j in range(OWN):
        at = slice(j * BLK, (j + 1) * BLK)
        seen = sum(ref[at, :].astype(F32) for ref in parts)
        spread = seen * columns[:, j : j + 1]
        gram += lax.dot_general(
            spread, spread, (((0,), (0,)), ((), ())), precision=HIGHEST, preferred_element_type=F32
        )
        pull += jnp.sum(spread * columns[:, OWN + j : OWN + j + 1], axis=0, keepdims=True)
    core = core_ref[0]
    zero, one = pack(gram, pull)
    keep_ref[...] = jnp.where(core == 0, zero, one)
    send_ref[...] = jnp.where(core == 0, one, zero)


def gram_halves(core, count, parts, values, weight):
    out = jax.ShapeDtypeStruct((BLK // 4 + 8, BLK), F32)
    return pl.pallas_call(
        gram_kernel,
        in_specs=[pl.BlockSpec(memory_space=SMEM)] * 2 + [pl.BlockSpec(memory_space=VMEM)] * 6,
        out_specs=[pl.BlockSpec(memory_space=VMEM)] * 2,
        out_shape=[out] * 2,
        compiler_params=pltpu.CompilerParams(vmem_limit_bytes=32 * 2**20),
        name="gram",
    )(core, count, *parts, values, weight)


PANEL = 32
SLABS = PANEL // 8


def invert_factor(rows):
    sub = [lax.broadcasted_iota(jnp.int32, (8, BLK), 0) + 8 * r for r in range(SLABS)]
    lane = lax.broadcasted_iota(jnp.int32, (8, BLK), 1)
    rows = list(rows)
    done = []
    for p in range(BLK // PANEL):
        at = PANEL * p
        slab = rows[SLABS * p : SLABS * (p + 1)]
        cols = [
            [jnp.broadcast_to(part[:, at + j : at + j + 1], (8, BLK)) for part in slab] for j in range(PANEL)
        ]
        inside = (lane >= at) & (lane < at + PANEL)
        slab = [
            jnp.where(inside, jnp.where(lane - at == sub[r], 1.0, 0.0), slab[r]) for r in range(SLABS)
        ]
        result = [jnp.zeros((8, BLK), F32)] * SLABS
        for t in range(PANEL):
            first, place_in = t // 8, t % 8
            scale = lax.rsqrt(jnp.broadcast_to(cols[t][first][place_in : place_in + 1], (8, BLK)))
            factor = [None] * SLABS
            for r in range(first, SLABS):
                factor[r] = cols[t][r] * scale
            factor[first] = jnp.where(sub[first] > t, factor[first], 0.0)
            for j in range(t + 1, PANEL):
                top = jnp.broadcast_to(factor[j // 8][j % 8 : j % 8 + 1], (8, BLK))
                for r in range(j // 8, SLABS):
                    cols[j][r] = cols[j][r] - factor[r] * top
            top = jnp.broadcast_to(slab[first][place_in : place_in + 1], (8, BLK)) * scale
            result[first] = jnp.where(sub[first] == t, top, result[first])
            for r in range(first, SLABS):
                slab[r] = slab[r] - factor[r] * top
        done += [jnp.where(lane <= sub[r] + at, result[r], 0.0) for r in range(SLABS)]
        if at + PANEL < BLK:
            full = jnp.concatenate(result, axis=0)
            outer = lax.dot_general(
                full, full, (((0,), (0,)), ((), ())), precision=HIGHEST, preferred_element_type=F32
            )
            for q in range(SLABS * (p + 1), BLK // 8):
                rows[q] = jnp.where(inside, 0.0, rows[q]) - outer[8 * q : 8 * q + 8]
    return done


CHUNK = 512
CHUNKS = LEVS * CELLS // CHUNK


def analysis_kernel(
    core_ref, mine_ref, other_ref, members_hbm, out_ref, transform_ref, members_ref, result, in_sem, out_sem
):
    load = pltpu.make_async_copy(members_hbm, members_ref, in_sem)
    load.start()
    core = core_ref[0]
    mine, other = mine_ref[...], other_ref[...]
    whole, pull = unpack(jnp.where(core == 0, mine, other), jnp.where(core == 0, other, mine))
    sub = lax.broadcasted_iota(jnp.int32, (8, BLK), 0)
    lane = lax.broadcasted_iota(jnp.int32, (8, BLK), 1)
    slabs = [
        whole[8 * p : 8 * p + 8, :] + jnp.where(lane == sub + 8 * p, 1.0, 0.0) for p in range(BLK // 8)
    ]
    inverse = jnp.concatenate(invert_factor(slabs), axis=0)
    inner = jnp.sum(inverse * pull, axis=1, keepdims=True)
    shift = jnp.sum(inverse * inner, axis=0, keepdims=True)
    transform = jnp.transpose(inverse + shift * (1.0 / math.sqrt(BLK - 1)))
    transform_ref[...] = transform
    rounded = transform.astype(BF)
    average = jnp.full((BLK, BLK), 1.0 / BLK, BF)
    load.wait()
    copies = []
    for n in range(CHUNKS):
        at = slice(n * CHUNK, (n + 1) * CHUNK)
        value = members_ref[at, :]
        row_mean = jnp.dot(value, average, preferred_element_type=F32)
        anomalies = (value.astype(F32) - row_mean).astype(BF)
        moved = jnp.dot(anomalies, rounded, preferred_element_type=F32)
        result[at, :] = (row_mean + moved).astype(BF)
        copies.append(pltpu.make_async_copy(result.at[at, :], out_ref.at[at, :], out_sem.at[n]))
        copies[-1].start()
    for copy in copies:
        copy.wait()


def analysis(core, mine, other, members):
    return pl.pallas_call(
        analysis_kernel,
        in_specs=[
            pl.BlockSpec(memory_space=SMEM),
            pl.BlockSpec(memory_space=VMEM),
            pl.BlockSpec(memory_space=VMEM),
            pl.BlockSpec(memory_space=HBM),
        ],
        out_specs=[pl.BlockSpec(memory_space=HBM), pl.BlockSpec(memory_space=VMEM)],
        out_shape=[
            jax.ShapeDtypeStruct((LEVS * CELLS, BLK), BF),
            jax.ShapeDtypeStruct((BLK, BLK), F32),
        ],
        scratch_shapes=[
            pltpu.VMEM((LEVS * CELLS, BLK), BF),
            pltpu.VMEM((LEVS * CELLS, BLK), BF),
            pltpu.SemaphoreType.DMA,
            pltpu.SemaphoreType.DMA((CHUNKS,)),
        ],
        compiler_params=pltpu.CompilerParams(vmem_limit_bytes=32 * 2**20),
        name="analysis",
    )(core, mine, other, members)


def shards(members, obs_operator, col_level, col_block, obs_count, obs_values, obs_weight):
    lev = lax.axis_index("lev").astype(jnp.int32)
    core = (lev % 2).reshape(1)
    x = (lev // 2).reshape(1)
    flat = members.reshape(LEVS * CELLS, BLK)

    up = [(i, i + 1) for i in range(31)]
    down = [(i + 1, i) for i in range(31)]
    before = lax.ppermute(members[:, CELLS - RIM :], "tile", up)
    after = lax.ppermute(members[:, :RIM], "tile", down)

    places = jnp.transpose(col_level * 32 + col_block, (0, 2, 1))
    send, keep, edge, rim = inner_blocks(core, places, obs_operator, flat)
    send, before, after = lax.optimization_barrier((send, before, after))
    came = other_core(send)
    send_edge, keep_edge = outer_blocks(core, places, edge, rim, before, after)
    own, *far = pair_sum(core, x, came, keep, other_core(send_edge), keep_edge)
    parts = [own] + [x_shift(far[k - 1], k) for k in (1, 2, 3)]

    send, keep = gram_halves(core, obs_count, parts, obs_values, obs_weight)
    total = keep + other_core(send)
    total = group_sum(total, PLANES)
    total = group_sum(total, LINES)
    other = other_core(total)

    analysed, transform = analysis(core, total, other, flat)
    return (analysed.reshape(LEVS, CELLS, BLK), transform)


def solution(mesh):
    placed = (
        P("lev", "tile", None),
        P("lev", "tile", None, None, None),
        P("lev", "tile", None),
        P("lev", "tile", None),
        P(("tile", "lev")),
        P(("tile", "lev"), None),
        P(("tile", "lev"), None),
    )
    return jax.shard_map(
        shards, mesh=mesh, in_specs=placed, out_specs=(P("lev", "tile", None), P()), check_vma=False
    )
```
